32 devices in a mesh: ctx: 8 (over z, y), head: 4 (over x, core).
Axes of the slice: x: 2, y: 2, z: 4, core: 2. Of those that a mesh axis runs over, the one named last changes fastest.
Arguments:
- query: bfloat16 [1024, 32, 128], P('ctx', 'head'), may hold values from -6 to 6
- key: bfloat16 [1024, 4, 128], P(('ctx', 'head')), may hold values from -6 to 6
- value: bfloat16 [1024, 4, 128], P(('ctx', 'head')), may hold values from -6 to 6
- d_out: bfloat16 [1024, 32, 128], P('ctx', 'head'), may hold values from -6 to 6
- seg_blocks: int32 [4], replicated, may hold values from 1 to 4, 8 in all
- seg_audio: int32 [4], replicated, may hold values 0 or 1
Outputs:
- d_query: bfloat16 [1024, 32, 128], P('ctx', 'head')
- d_key: bfloat16 [1024, 4, 128], P(('ctx', 'head'))
- d_value: bfloat16 [1024, 4, 128], P(('ctx', 'head'))
The draws below stay inside these ranges and needn't reach their ends.
Inputs may be any that keep to these rules, and one draw needn't show every extreme that they name: `seg_blocks`: the segments tile the 8 blocks in order: their lengths sum to 8.
All inputs are finite; a program needn't handle non-finite values.
Results may differ from the reference program's by a relative error of at most 0.0055.
Values may be sent and summed in bfloat16 or wider, within the bound.
A program may use at most 128 MiB of HBM per device.

```python
import math
import jax
import jax.numpy as jnp
import numpy as np
from jax import lax

DH = 128
GROUP = 8
KVH = 4
HQ = 32
BLK = 128
MOST = 4
L = 1024
NB = 8
NSEG = 4


def draw_query(key, part):
    entries = jax.random.truncated_normal(jax.random.fold_in(key, 3), -6.0, 6.0, (L, HQ, DH), jnp.float32)
    return entries.astype(jnp.bfloat16)


def draw_key(key, part):
    entries = jax.random.truncated_normal(jax.random.fold_in(key, 5), -6.0, 6.0, (L, KVH, DH), jnp.float32)
    return entries.astype(jnp.bfloat16)


def plant(values, rng, smallest, top_value):
    index_at = [jax.random.randint(jax.random.fold_in(rng, axis), (), 0, length) for axis, length in enumerate(values.shape)]
    main_axis = values.shape.index(max(values.shape))
    next_to = index_at[:main_axis] + [(index_at[main_axis] + 1) % values.shape[main_axis]] + index_at[main_axis + 1:]
    return values.at[tuple(index_at)].set(smallest).at[tuple(next_to)].set(top_value)


def block_scale(key, extent, split, low, high):
    gain, own = 1.0, jax.random.fold_in(key, 6)
    for dim, shards_of in split:
        heights = jnp.exp(jax.random.uniform(jax.random.fold_in(own, dim), (shards_of,), jnp.float32, low / len(split), high / len(split)))
        gain = gain * jnp.repeat(heights, extent[dim] // shards_of).reshape([-1 if axis == dim else 1 for axis in range(len(extent))])
    return gain


def split_up(count, total, bound, skew):
    weights = [(1 << 20) // math.isqrt(rank ** skew) + 1 for rank in range(2, count + 1)]
    surplus, given = total - bound - (count - 1), [1] * (count - 1)
    while surplus > 0:
        free = [i for i in range(count - 1) if given[i] < bound]
        whole, budget = sum([weights[i] for i in free]), surplus
        for i in free:
            addition = min(bound - given[i], max(1, budget * weights[i] // whole), surplus)
            given[i] = given[i] + addition
            surplus = surplus - addition
    return np.array([bound] + given)


def uneven_parts(own_key, number_of, total, reach, slope):
    if number_of == 2:
        one = jax.random.randint(own_key, (), max(1, total - reach), min(reach, total - 1) + 1)
        return jnp.stack([one, total - one])
    tallies = jnp.asarray(split_up(number_of, total, reach, slope), jnp.int32)
    couples = (number_of - 1) // 2
    giver, sink = tallies[1:1 + 2 * couples:2], tallies[2:2 + 2 * couples:2]
    room = jnp.minimum(giver - 1, reach - sink)
    moved = jax.random.randint(jax.random.fold_in(own_key, 1), (couples,), 0, 1 << 20) % (room + 1)
    tallies = tallies.at[1:1 + 2 * couples:2].set(giver - moved).at[2:2 + 2 * couples:2].set(sink + moved)
    return tallies[jax.random.permutation(jax.random.fold_in(own_key, 2), number_of)]


def bell_draw(stream_key, dims, width, most, pieces=(), kind=jnp.bfloat16):
    values = jax.random.normal(stream_key, dims, jnp.float32) * width
    if len(pieces) > 0:
        values = block_scale(stream_key, dims, pieces, -0.22, 0.18) * values
    return jnp.clip(values, min=-most, max=most).astype(kind)


def setup_inputs(seed: int = 0) -> dict:
    splits = jax.random.split(jax.random.key(seed), 7)
    return {
        "query": draw_query(jax.random.fold_in(splits[6], 71), 0),
        "key": draw_key(jax.random.fold_in(splits[6], 71), 0),
        "value": bell_draw(splits[2], (L, KVH, DH), 1.0, 6.0, ((0, 32),)),
        "d_out": bell_draw(splits[3], (L, HQ, DH), 1.0, 6.0, ((0, 8), (1, 4))),
        "seg_blocks": uneven_parts(splits[4], NSEG, NB, MOST, 1).astype(jnp.int32),
        "seg_audio": plant((jax.random.randint(splits[5], (NSEG,), 0, 2) < 1).astype(jnp.int32), jax.random.fold_in(splits[5], 1), 0, 1),
    }


NEG = -1e+30

def segment_tables(seg_blocks, seg_audio, positions):
    ends = jnp.cumsum(seg_blocks).astype(jnp.int32)
    starts = (ends - seg_blocks).astype(jnp.int32)
    blocks = (positions // BLK).astype(jnp.int32)
    inside = (starts[None, :] <= blocks[:, None]) & (blocks[:, None] < ends[None, :])
    numbers = jnp.arange(seg_blocks.shape[0], dtype=jnp.int32)
    segment = lax.optimization_barrier(jnp.sum(jnp.where(inside, numbers[None, :], 0), axis=1)).astype(jnp.int32)
    audio = lax.optimization_barrier(jnp.sum(jnp.where(inside, seg_audio[None, :], 0), axis=1)).astype(jnp.int32)
    return (segment, audio)

def visible(query_pos, key_pos, query_seg, query_audio, key_seg):
    causal = key_pos[None, :] <= query_pos[:, None]
    span = (query_seg[:, None] == key_seg[None, :]) & (query_audio[:, None] == 1)
    return causal | span

def reference(query, key, value, d_out, seg_blocks, seg_audio):
    total = query.shape[0]
    count = total // BLK
    scale = 1.0 / math.sqrt(DH)
    positions = jnp.arange(total, dtype=jnp.int32)
    segment, audio = segment_tables(seg_blocks, seg_audio, positions)
    grads_query, grads_key, grads_value = ([], [], [])
    for group_head in range(KVH):
        keys = key[:, group_head, :]
        values = value[:, group_head, :]
        lower = group_head * GROUP
        query_blocks = query[:, lower:lower + GROUP, :].reshape(count, BLK * GROUP, DH)
        out_blocks = d_out[:, lower:lower + GROUP, :].reshape(count, BLK * GROUP, DH)
        inputs = (query_blocks, out_blocks, positions.reshape(count, BLK), segment.reshape(count, BLK), audio.reshape(count, BLK))

        def step(carry, block_inputs):
            key_grad, value_grad = carry
            query_rows, out_rows, query_pos, query_seg, query_audio = block_inputs
            mask = visible(query_pos, positions, query_seg, query_audio, segment)[:, None, :]
            scores = (jnp.dot(query_rows, keys.T, preferred_element_type=jnp.float32) * scale).reshape(BLK, GROUP, total)
            highest = lax.optimization_barrier(jnp.max(jnp.where(mask, scores, NEG), axis=2, keepdims=True))
            lse = highest + jnp.log(lax.optimization_barrier(jnp.sum(jnp.where(mask, jnp.exp(scores - highest), 0.0), axis=2, keepdims=True)))
            probs = jnp.where(mask, jnp.exp(scores - lse), 0.0)
            d_probs = jnp.dot(out_rows, values.T, preferred_element_type=jnp.float32).reshape(BLK, GROUP, total)
            delta = lax.optimization_barrier(jnp.sum(probs * d_probs, axis=2, keepdims=True))
            probs_low = probs.astype(jnp.bfloat16).reshape(BLK * GROUP, total)
            d_scores = (probs * (d_probs - delta)).astype(jnp.bfloat16).reshape(BLK * GROUP, total)
            value_grad = value_grad + jnp.dot(probs_low.T, out_rows, preferred_element_type=jnp.float32)
            key_grad = key_grad + jnp.dot(d_scores.T, query_rows, preferred_element_type=jnp.float32)
            grad_rows = (jnp.dot(d_scores, keys, preferred_element_type=jnp.float32) * scale).astype(jnp.bfloat16)
            return ((key_grad, value_grad), grad_rows)
        zeros = jnp.zeros((total, DH), jnp.float32)
        (key_grad, value_grad), grad_rows = lax.scan(step, (zeros, zeros), inputs)
        grads_query.append(grad_rows.reshape(total, GROUP, DH))
        grads_key.append((key_grad * scale).astype(jnp.bfloat16))
        grads_value.append(value_grad.astype(jnp.bfloat16))
    return (jnp.concatenate(grads_query, axis=1), jnp.stack(grads_key, axis=1), jnp.stack(grads_value, axis=1))
```

```python
import functools
import math

import jax
import jax.numpy as jnp
from jax import lax
from jax.experimental import pallas as pl
from jax.experimental.pallas import tpu as pltpu
from jax.sharding import PartitionSpec as P

MESH = pl.DeviceIdType.MESH
VMEM_BUDGET = 48 * 2**20
ROW_CHUNK = 256

DH = 128
GROUP = 8
BLK = 128


NEG = -1e30


def segment_tables(seg_blocks, seg_audio, positions):
    ends = jnp.cumsum(seg_blocks)
    starts = ends - seg_blocks
    blocks = positions // BLK
    inside = (starts[None, :] <= blocks[:, None]) & (blocks[:, None] < ends[None, :])
    numbers = jnp.arange(seg_blocks.shape[0], dtype=jnp.int32)
    segment = jnp.sum(jnp.where(inside, numbers[None, :], 0), axis=1)
    audio = jnp.sum(jnp.where(inside, seg_audio[None, :], 0), axis=1)
    return (segment, audio)


def visible(query_pos, key_pos, query_seg, query_audio, key_seg):
    causal = key_pos[None, :] <= query_pos[:, None]
    span = (query_seg[:, None] == key_seg[None, :]) & (query_audio[:, None] == 1)
    return causal | span


def prepare(rows_query, rows_out, query_pos, seg_blocks, seg_audio):
    tokens = rows_query.shape[0]
    query_seg, query_audio = segment_tables(seg_blocks, seg_audio, query_pos)
    query_flat = rows_query.reshape(tokens * GROUP, DH)
    out_flat = rows_out.reshape(tokens * GROUP, DH)
    return (query_flat, out_flat, query_pos, query_seg, query_audio)


def piece_mask(group_data, keys, seg_blocks, seg_audio):
    query_flat, out_flat, query_pos, query_seg, query_audio = group_data
    key_pos = jnp.arange(keys.shape[0], dtype=jnp.int32)
    key_seg = segment_tables(seg_blocks, seg_audio, key_pos)[0]
    return visible(query_pos, key_pos, query_seg, query_audio, key_seg)


def contract_rows(left, right):
    return lax.dot_general(
        left, right, (((1,), (1,)), ((), ())), preferred_element_type=jnp.float32
    )


def contract_first(left, right):
    return lax.dot_general(
        left, right, (((0,), (0,)), ((), ())), preferred_element_type=jnp.float32
    )


def stats_group(group_data, state, piece, seg_blocks, seg_audio):
    query_flat, out_flat, query_pos, query_seg, query_audio = group_data
    keys, values = piece
    count = keys.shape[0]
    tokens = query_pos.shape[0]
    scale = 1.0 / math.sqrt(DH)
    mask = piece_mask(group_data, keys, seg_blocks, seg_audio)

    def stats_compute(kept):
        highest, total, weighted = kept
        wide = mask[:, None, :]
        scores = (contract_rows(query_flat, keys) * scale).reshape(tokens, GROUP, count)
        new_high = jnp.maximum(highest, jnp.max(jnp.where(wide, scores, NEG), axis=2))
        probs = jnp.where(wide, jnp.exp(scores - new_high[:, :, None]), 0.0)
        d_probs = contract_rows(out_flat, values).reshape(tokens, GROUP, count)
        return (new_high, jnp.sum(probs, axis=2), jnp.sum(probs * d_probs, axis=2))

    def stats_skipped(kept):
        return kept

    return lax.cond(jnp.any(mask), stats_compute, stats_skipped, state)


def grad_group(group_data, finals, grad_rows, piece, seg_blocks, seg_audio):
    query_flat, out_flat, query_pos, query_seg, query_audio = group_data
    lse, delta = finals
    keys, values = piece
    count = keys.shape[0]
    tokens = query_pos.shape[0]
    scale = 1.0 / math.sqrt(DH)
    mask = piece_mask(group_data, keys, seg_blocks, seg_audio)

    def grad_compute(grad_rows):
        wide = mask[:, None, :]
        scores = (contract_rows(query_flat, keys) * scale).reshape(tokens, GROUP, count)
        probs = jnp.where(wide, jnp.exp(scores - lse[:, :, None]), 0.0)
        d_probs = contract_rows(out_flat, values).reshape(tokens, GROUP, count)
        probs_low = probs.astype(jnp.bfloat16).reshape(tokens * GROUP, count)
        d_scores = (
            (probs * (d_probs - delta[:, :, None]))
            .astype(jnp.bfloat16)
            .reshape(tokens * GROUP, count)
        )
        value_part = contract_first(probs_low, out_flat)
        key_part = contract_first(d_scores, query_flat)
        grad_rows = jnp.dot(d_scores, keys, preferred_element_type=jnp.float32)
        return (grad_rows, key_part, value_part)

    def grad_skipped(grad_rows):
        blank = jnp.zeros((count, keys.shape[1]), jnp.float32)
        return (grad_rows, blank, blank)

    return lax.cond(jnp.any(mask), grad_compute, grad_skipped, grad_rows)


def body(query, key, value, d_out, seg_blocks, seg_audio):
    key, value = (
        lax.all_to_all(key, "head", split_axis=1, concat_axis=0, tiled=True),
        lax.all_to_all(value, "head", split_axis=1, concat_axis=0, tiled=True),
    )
    rows = query.shape[0]
    half = rows // 2
    place = lax.axis_index("ctx")
    scale = 1.0 / math.sqrt(DH)
    keys = key[:, 0, :]
    values = value[:, 0, :]
    own_pos = place * rows + jnp.arange(rows, dtype=jnp.int32)
    first = prepare(query[:half], d_out[:half], own_pos[:half], seg_blocks, seg_audio)
    second = prepare(query[half:], d_out[half:], own_pos[half:], seg_blocks, seg_audio)
    groups = (first, second)
    blank_stats = jnp.zeros((half, GROUP), jnp.float32)
    start_stats = tuple(
        (
            (jnp.full((half, GROUP), NEG, jnp.float32), blank_stats, blank_stats)
            for group_data in groups
        )
    )
    piece = (
        lax.all_gather(keys, "ctx", axis=0, tiled=True),
        lax.all_gather(values, "ctx", axis=0, tiled=True),
    )
    stats = tuple(
        (
            stats_group(group_data, state, piece, seg_blocks, seg_audio)
            for group_data, state in zip(groups, start_stats)
        )
    )
    finals = tuple(
        ((highest + jnp.log(total), weighted / total) for highest, total, weighted in stats)
    )
    blank_rows = jnp.zeros((half * GROUP, DH), jnp.float32)
    piece = (
        lax.all_gather(keys, "ctx", axis=0, tiled=True),
        lax.all_gather(values, "ctx", axis=0, tiled=True),
    )
    grad_list = (blank_rows, blank_rows)
    piece_keys = piece[0]
    count = piece_keys.shape[0]
    key_sum = jnp.zeros((count, DH), jnp.float32)
    value_sum = jnp.zeros((count, DH), jnp.float32)
    new_rows = []
    for group_data, group_finals, grad_rows in zip(groups, finals, grad_list):
        grad_rows, key_part, value_part = grad_group(
            group_data, group_finals, grad_rows, piece, seg_blocks, seg_audio
        )
        key_sum = key_sum + key_part
        value_sum = value_sum + value_part
        new_rows.append(grad_rows)
    update = jnp.stack([key_sum, value_sum], axis=1)
    key_grad = update
    grads = (key_grad, tuple(new_rows))
    key_grad, grad_list = grads
    summed = lax.psum_scatter(key_grad, "ctx", scatter_dimension=0, tiled=True)
    d_key = (summed[:, 0, :] * scale).astype(jnp.bfloat16)[:, None, :]
    d_value = summed[:, 1, :].astype(jnp.bfloat16)[:, None, :]
    first_rows = (grad_list[0] * scale).astype(jnp.bfloat16).reshape(half, GROUP, DH)
    second_rows = (grad_list[1] * scale).astype(jnp.bfloat16).reshape(half, GROUP, DH)
    d_query = jnp.concatenate([first_rows, second_rows], axis=0)
    d_key, d_value = (
        lax.all_to_all(d_key, "head", split_axis=0, concat_axis=1, tiled=True),
        lax.all_to_all(d_value, "head", split_axis=0, concat_axis=1, tiled=True),
    )
    return (d_query, d_key, d_value)


def fused_kernel(
    n, heads, q_ref, do_ref, k_ref, v_ref, blocks_ref, audio_ref,
    dq_ref, dk_ref, dv_ref,
    head_out, kv, p_s, dp_s, ds_s, m_s, l_s, w_s, own_part,
    gy_out, gy_in, gz_out, gz_in, fin_out, fin_in,
    h_send, h_recv, kv_recv, kvz_send, kvy_send,
    gy_send, gy_recv, gz_send, gz_recv, f_send, f_recv,
):
    chain = n // 2
    place = lax.axis_index("ctx")
    head = lax.axis_index("head")
    a, b = place // 2, lax.rem(place, 2)
    rows_flat = q_ref.shape[0]
    rows = rows_flat // GROUP
    part = rows // heads
    scale = 1.0 / math.sqrt(DH)
    power = scale * math.log2(math.e)
    chunk = min(ROW_CHUNK, rows_flat)
    chunks = [slice(r, r + chunk) for r in range(0, rows_flat, chunk)]

    def head_peer(d):
        return lax.rem(head + d, heads)

    def up(d):
        return lax.rem(a + d, chain)

    def down(d):
        return lax.rem(a + chain - d, chain)

    def at(ctx_index, head_index):
        return (ctx_index, head_index)

    partner = 2 * a + 1 - b

    def send(src, dst, send_sem, recv_sem, target):
        return pltpu.make_async_remote_copy(
            src_ref=src, dst_ref=dst, send_sem=send_sem, recv_sem=recv_sem,
            device_id=target, device_id_type=MESH,
        )

    barrier = pltpu.get_barrier_semaphore()
    for d in range(1, heads):
        pl.semaphore_signal(barrier, inc=1, device_id=at(place, head_peer(d)), device_id_type=MESH)
    pl.semaphore_signal(barrier, inc=1, device_id=at(partner, head), device_id_type=MESH)
    for d in range(1, chain):
        pl.semaphore_signal(barrier, inc=1, device_id=at(2 * up(d) + b, head), device_id_type=MESH)

    for i in range(heads):
        head_out[i, 0] = k_ref[:, i, :]
        head_out[i, 1] = v_ref[:, i, :]
    pl.semaphore_wait(barrier, heads - 1 + chain)

    mine = pl.ds(pl.multiple_of(head * part, part), part)

    def head_copy(d):
        peer = head_peer(d)
        return send(head_out.at[peer], kv.at[place, :, mine, :], h_send.at[d], h_recv.at[d], at(place, peer))

    for d in range(1, heads):
        head_copy(d).start()
    kv[place, :, mine, :] = head_out[head]

    pos = place * rows + lax.broadcasted_iota(jnp.int32, (1, rows_flat), 1) // GROUP
    limit = pos + 1
    start = jnp.int32(0)
    for s in range(blocks_ref.shape[0]):
        end = start + blocks_ref[s] * BLK
        inside = (pos >= start) & (pos < end) & (jnp.broadcast_to(audio_ref[s], pos.shape) == 1)
        limit = jnp.where(inside, end, limit)
        start = end

    for d in range(1, heads):
        head_copy(d).wait_recv()

    def chain_copy(d):
        return send(kv.at[place], kv.at[place], kvz_send.at[d], kv_recv.at[place], at(2 * up(d) + b, head))

    def relay_copy(d):
        slot = 2 * down(d) + b
        return send(kv.at[slot], kv.at[slot], kvy_send.at[d], kv_recv.at[slot], at(partner, head))

    relay_copy(0).start()
    for d in range(1, chain):
        chain_copy(d).start()

    def stats_step(t, carry):
        d = t // 2
        own_column = lax.rem(t, 2) == 0
        slot = 2 * down(d) + lax.rem(b + t, 2)

        @pl.when(t > 0)
        def _():
            send(kv.at[slot], kv.at[slot], kvy_send.at[d], kv_recv.at[slot], at(partner, head)).wait_recv()

        @pl.when(own_column & (t > 0))
        def _():
            relay_copy(d).start()

        keys, values = kv[slot, 0], kv[slot, 1]
        key_pos = slot * rows + lax.broadcasted_iota(jnp.int32, (rows, 1), 0)
        for c in chunks:
            s = contract_rows(keys, q_ref[c, :])
            s = jnp.where(key_pos < limit[:, c], s, NEG)
            high = jnp.max(s, axis=0, keepdims=True)
            p = jnp.exp2((s - high) * power)
            dp = contract_rows(values, do_ref[c, :])
            p_s[slot, :, c] = p
            dp_s[slot, :, c] = dp
            m_s[slot, :, c] = high
            l_s[slot, :, c] = jnp.sum(p, axis=0, keepdims=True)
            w_s[slot, :, c] = jnp.sum(p * dp, axis=0, keepdims=True)
        return carry

    lax.fori_loop(0, n, stats_step, 0)

    m_all = m_s[...]
    high = jnp.max(m_all, axis=0)
    factors = jnp.exp2((m_all - high[None]) * power)
    total = jnp.sum(factors * l_s[...], axis=0)
    delta = jnp.sum(factors * w_s[...], axis=0) / total
    m_s[...] = factors / total[None]

    def pair_copy(d):
        dest = down(d)
        return send(gy_out.at[d], gy_in.at[dest], gy_send.at[d], gy_recv.at[dest], at(partner, head))

    def sum_copy(d):
        return send(gz_out.at[d], gz_in.at[a], gz_send.at[d], gz_recv.at[a], at(2 * down(d) + b, head))

    def combine(d):
        pair_copy(d).wait_recv()
        return own_part[d] + gy_in[down(d)].astype(jnp.float32)

    def grad_step(t, carry):
        d = lax.rem(t // 2 + 1, chain)
        other_column = lax.rem(t, 2) == 0
        slot = 2 * down(d) + lax.rem(b + t + 1, 2)
        key_part = jnp.zeros((rows, DH), jnp.float32)
        value_part = jnp.zeros((rows, DH), jnp.float32)
        for c in chunks:
            probs = p_s[slot, :, c] * m_s[slot, :, c]
            ds = (probs * (dp_s[slot, :, c] - delta[:, c])).astype(jnp.bfloat16)
            ds_s[slot, :, c] = ds
            value_part += jnp.dot(probs.astype(jnp.bfloat16), do_ref[c, :], preferred_element_type=jnp.float32)
            key_part += jnp.dot(ds, q_ref[c, :], preferred_element_type=jnp.float32)

        @pl.when(other_column)
        def _():
            gy_out[d, 0] = key_part.astype(jnp.bfloat16)
            gy_out[d, 1] = value_part.astype(jnp.bfloat16)
            pair_copy(d).start()

        @pl.when(jnp.logical_not(other_column))
        def _():
            own_part[d, 0] = key_part
            own_part[d, 1] = value_part

        @pl.when(jnp.logical_not(other_column) & (t > 1))
        def _():
            before = t // 2
            gz_out[before] = combine(before).astype(jnp.bfloat16)
            sum_copy(before).start()

        return carry

    lax.fori_loop(0, n, grad_step, 0)

    all_keys = kv[:, 0].reshape(n * rows, DH)
    all_ds = ds_s[...].reshape(n * rows, rows_flat)
    dq = contract_first(all_keys, all_ds) * scale
    dq_ref[...] = dq.T.astype(jnp.bfloat16)

    acc = combine(0)
    for d in range(1, chain):
        source = up(d)
        send(gz_out.at[d], gz_in.at[source], gz_send.at[d], gz_recv.at[source], at(2 * down(d) + b, head)).wait_recv()
        acc = acc + gz_in[source].astype(jnp.float32)
    fin_out[0] = (acc[0] * scale).astype(jnp.bfloat16)
    fin_out[1] = acc[1].astype(jnp.bfloat16)

    def final_copy(d):
        peer = head_peer(d)
        theirs = pl.ds(pl.multiple_of(peer * part, part), part)
        return send(fin_out.at[:, theirs, :], fin_in.at[head], f_send.at[d], f_recv.at[d], at(place, peer))

    for d in range(1, heads):
        final_copy(d).start()
    fin_in[head] = fin_out[:, mine, :]
    for d in range(1, heads):
        final_copy(d).wait_recv()
    for i in range(heads):
        dk_ref[:, i, :] = fin_in[i, 0]
        dv_ref[:, i, :] = fin_in[i, 1]

    for d in range(1, heads):
        head_copy(d).wait_send()
        final_copy(d).wait_send()
    for d in range(chain):
        relay_copy(d).wait_send()
        pair_copy(d).wait_send()
    for d in range(1, chain):
        chain_copy(d).wait_send()
        sum_copy(d).wait_send()


def fused_scratch(n, heads, rows):
    flat, chain, part = rows * GROUP, n // 2, rows // heads
    low, full, sem = jnp.bfloat16, jnp.float32, pltpu.SemaphoreType.DMA
    return [
        pltpu.VMEM((heads, 2, part, DH), low),
        pltpu.VMEM((n, 2, rows, DH), low),
        pltpu.VMEM((n, rows, flat), full),
        pltpu.VMEM((n, rows, flat), full),
        pltpu.VMEM((n, rows, flat), low),
        pltpu.VMEM((n, 1, flat), full),
        pltpu.VMEM((n, 1, flat), full),
        pltpu.VMEM((n, 1, flat), full),
        pltpu.VMEM((chain, 2, rows, DH), full),
        pltpu.VMEM((chain, 2, rows, DH), low),
        pltpu.VMEM((chain, 2, rows, DH), low),
        pltpu.VMEM((chain, 2, rows, DH), low),
        pltpu.VMEM((chain, 2, rows, DH), low),
        pltpu.VMEM((2, rows, DH), low),
        pltpu.VMEM((heads, 2, part, DH), low),
        sem((heads,)), sem((heads,)), sem((n,)), sem((chain,)), sem((chain,)),
        sem((chain,)), sem((chain,)), sem((chain,)), sem((chain,)), sem((heads,)), sem((heads,)),
    ]


def fused_body(n, heads, query, key, value, d_out, seg_blocks, seg_audio):
    rows = query.shape[0]
    flat = rows * GROUP
    low = jnp.bfloat16
    vmem, smem = pl.BlockSpec(memory_space=pltpu.VMEM), pl.BlockSpec(memory_space=pltpu.SMEM)
    d_query, d_key, d_value = pl.pallas_call(
        functools.partial(fused_kernel, n, heads),
        out_shape=[
            jax.ShapeDtypeStruct((flat, DH), low),
            jax.ShapeDtypeStruct(key.shape, low),
            jax.ShapeDtypeStruct(value.shape, low),
        ],
        in_specs=[vmem] * 4 + [smem] * 2,
        out_specs=[vmem] * 3,
        scratch_shapes=fused_scratch(n, heads, rows),
        cost_estimate=pl.CostEstimate(
            flops=10 * n * rows * flat * DH, bytes_accessed=6 * flat * DH, transcendentals=n * rows * flat
        ),
        compiler_params=pltpu.CompilerParams(
            collective_id=0, has_side_effects=True, vmem_limit_bytes=VMEM_BUDGET
        ),
    )(query.reshape(flat, DH), d_out.reshape(flat, DH), key, value, seg_blocks, seg_audio)
    return d_query.reshape(query.shape), d_key, d_value


def plan_body(n, heads, query, key, value, d_out, seg_blocks, seg_audio):
    rows = query.shape[0]
    held = n * rows * rows * GROUP * 10
    if held > VMEM_BUDGET // 2 or n % 2 or query.shape[1] != GROUP or key.shape[1] != heads:
        return body(query, key, value, d_out, seg_blocks, seg_audio)
    return fused_body(n, heads, query, key, value, d_out, seg_blocks, seg_audio)


def solution(mesh):
    placed = (
        P("ctx", "head", None),
        P(("ctx", "head"), None, None),
        P(("ctx", "head"), None, None),
        P("ctx", "head", None),
        P(),
        P(),
    )
    return jax.shard_map(
        functools.partial(plan_body, mesh.shape["ctx"], mesh.shape["head"]),
        mesh=mesh,
        in_specs=placed,
        out_specs=(
            P("ctx", "head", None),
            P(("ctx", "head"), None, None),
            P(("ctx", "head"), None, None),
        ),
        check_vma=False,
    )
```

```python
import functools
import math

import jax
import jax.numpy as jnp
from jax import lax
from jax.experimental import pallas as pl
from jax.experimental.pallas import tpu as pltpu
from jax.sharding import PartitionSpec as P

MESH = pl.DeviceIdType.MESH
VMEM_BUDGET = 60 * 2**20
ROW_CHUNK = 256

DH = 128
GROUP = 8
BLK = 128


NEG = -1e30


def segment_tables(seg_blocks, seg_audio, positions):
    ends = jnp.cumsum(seg_blocks)
    starts = ends - seg_blocks
    blocks = positions // BLK
    inside = (starts[None, :] <= blocks[:, None]) & (blocks[:, None] < ends[None, :])
    numbers = jnp.arange(seg_blocks.shape[0], dtype=jnp.int32)
    segment = jnp.sum(jnp.where(inside, numbers[None, :], 0), axis=1)
    audio = jnp.sum(jnp.where(inside, seg_audio[None, :], 0), axis=1)
    return (segment, audio)


def visible(query_pos, key_pos, query_seg, query_audio, key_seg):
    causal = key_pos[None, :] <= query_pos[:, None]
    span = (query_seg[:, None] == key_seg[None, :]) & (query_audio[:, None] == 1)
    return causal | span


def prepare(rows_query, rows_out, query_pos, seg_blocks, seg_audio):
    tokens = rows_query.shape[0]
    query_seg, query_audio = segment_tables(seg_blocks, seg_audio, query_pos)
    query_flat = rows_query.reshape(tokens * GROUP, DH)
    out_flat = rows_out.reshape(tokens * GROUP, DH)
    return (query_flat, out_flat, query_pos, query_seg, query_audio)


def piece_mask(group_data, keys, seg_blocks, seg_audio):
    query_flat, out_flat, query_pos, query_seg, query_audio = group_data
    key_pos = jnp.arange(keys.shape[0], dtype=jnp.int32)
    key_seg = segment_tables(seg_blocks, seg_audio, key_pos)[0]
    return visible(query_pos, key_pos, query_seg, query_audio, key_seg)


def contract_rows(left, right):
    return lax.dot_general(
        left, right, (((1,), (1,)), ((), ())), preferred_element_type=jnp.float32
    )


def contract_first(left, right):
    return lax.dot_general(
        left, right, (((0,), (0,)), ((), ())), preferred_element_type=jnp.float32
    )


def stats_group(group_data, state, piece, seg_blocks, seg_audio):
    query_flat, out_flat, query_pos, query_seg, query_audio = group_data
    keys, values = piece
    count = keys.shape[0]
    tokens = query_pos.shape[0]
    scale = 1.0 / math.sqrt(DH)
    mask = piece_mask(group_data, keys, seg_blocks, seg_audio)

    def stats_compute(kept):
        highest, total, weighted = kept
        wide = mask[:, None, :]
        scores = (contract_rows(query_flat, keys) * scale).reshape(tokens, GROUP, count)
        new_high = jnp.maximum(highest, jnp.max(jnp.where(wide, scores, NEG), axis=2))
        probs = jnp.where(wide, jnp.exp(scores - new_high[:, :, None]), 0.0)
        d_probs = contract_rows(out_flat, values).reshape(tokens, GROUP, count)
        return (new_high, jnp.sum(probs, axis=2), jnp.sum(probs * d_probs, axis=2))

    def stats_skipped(kept):
        return kept

    return lax.cond(jnp.any(mask), stats_compute, stats_skipped, state)


def grad_group(group_data, finals, grad_rows, piece, seg_blocks, seg_audio):
    query_flat, out_flat, query_pos, query_seg, query_audio = group_data
    lse, delta = finals
    keys, values = piece
    count = keys.shape[0]
    tokens = query_pos.shape[0]
    scale = 1.0 / math.sqrt(DH)
    mask = piece_mask(group_data, keys, seg_blocks, seg_audio)

    def grad_compute(grad_rows):
        wide = mask[:, None, :]
        scores = (contract_rows(query_flat, keys) * scale).reshape(tokens, GROUP, count)
        probs = jnp.where(wide, jnp.exp(scores - lse[:, :, None]), 0.0)
        d_probs = contract_rows(out_flat, values).reshape(tokens, GROUP, count)
        probs_low = probs.astype(jnp.bfloat16).reshape(tokens * GROUP, count)
        d_scores = (
            (probs * (d_probs - delta[:, :, None]))
            .astype(jnp.bfloat16)
            .reshape(tokens * GROUP, count)
        )
        value_part = contract_first(probs_low, out_flat)
        key_part = contract_first(d_scores, query_flat)
        grad_rows = jnp.dot(d_scores, keys, preferred_element_type=jnp.float32)
        return (grad_rows, key_part, value_part)

    def grad_skipped(grad_rows):
        blank = jnp.zeros((count, keys.shape[1]), jnp.float32)
        return (grad_rows, blank, blank)

    return lax.cond(jnp.any(mask), grad_compute, grad_skipped, grad_rows)


def body(query, key, value, d_out, seg_blocks, seg_audio):
    key, value = (
        lax.all_to_all(key, "head", split_axis=1, concat_axis=0, tiled=True),
        lax.all_to_all(value, "head", split_axis=1, concat_axis=0, tiled=True),
    )
    rows = query.shape[0]
    half = rows // 2
    place = lax.axis_index("ctx")
    scale = 1.0 / math.sqrt(DH)
    keys = key[:, 0, :]
    values = value[:, 0, :]
    own_pos = place * rows + jnp.arange(rows, dtype=jnp.int32)
    first = prepare(query[:half], d_out[:half], own_pos[:half], seg_blocks, seg_audio)
    second = prepare(query[half:], d_out[half:], own_pos[half:], seg_blocks, seg_audio)
    groups = (first, second)
    blank_stats = jnp.zeros((half, GROUP), jnp.float32)
    start_stats = tuple(
        (
            (jnp.full((half, GROUP), NEG, jnp.float32), blank_stats, blank_stats)
            for group_data in groups
        )
    )
    piece = (
        lax.all_gather(keys, "ctx", axis=0, tiled=True),
        lax.all_gather(values, "ctx", axis=0, tiled=True),
    )
    stats = tuple(
        (
            stats_group(group_data, state, piece, seg_blocks, seg_audio)
            for group_data, state in zip(groups, start_stats)
        )
    )
    finals = tuple(
        ((highest + jnp.log(total), weighted / total) for highest, total, weighted in stats)
    )
    blank_rows = jnp.zeros((half * GROUP, DH), jnp.float32)
    piece = (
        lax.all_gather(keys, "ctx", axis=0, tiled=True),
        lax.all_gather(values, "ctx", axis=0, tiled=True),
    )
    grad_list = (blank_rows, blank_rows)
    piece_keys = piece[0]
    count = piece_keys.shape[0]
    key_sum = jnp.zeros((count, DH), jnp.float32)
    value_sum = jnp.zeros((count, DH), jnp.float32)
    new_rows = []
    for group_data, group_finals, grad_rows in zip(groups, finals, grad_list):
        grad_rows, key_part, value_part = grad_group(
            group_data, group_finals, grad_rows, piece, seg_blocks, seg_audio
        )
        key_sum = key_sum + key_part
        value_sum = value_sum + value_part
        new_rows.append(grad_rows)
    update = jnp.stack([key_sum, value_sum], axis=1)
    key_grad = update
    grads = (key_grad, tuple(new_rows))
    key_grad, grad_list = grads
    summed = lax.psum_scatter(key_grad, "ctx", scatter_dimension=0, tiled=True)
    d_key = (summed[:, 0, :] * scale).astype(jnp.bfloat16)[:, None, :]
    d_value = summed[:, 1, :].astype(jnp.bfloat16)[:, None, :]
    first_rows = (grad_list[0] * scale).astype(jnp.bfloat16).reshape(half, GROUP, DH)
    second_rows = (grad_list[1] * scale).astype(jnp.bfloat16).reshape(half, GROUP, DH)
    d_query = jnp.concatenate([first_rows, second_rows], axis=0)
    d_key, d_value = (
        lax.all_to_all(d_key, "head", split_axis=0, concat_axis=1, tiled=True),
        lax.all_to_all(d_value, "head", split_axis=0, concat_axis=1, tiled=True),
    )
    return (d_query, d_key, d_value)


def fused_kernel(
    n, heads, q_hbm, do_hbm, k_hbm, v_hbm, blocks_hbm, audio_hbm,
    dq_ref, dk_ref, dv_ref,
    q_ref, do_ref, k_ref, v_ref, blocks_ref, audio_ref, q_turned, do_turned,
    head_out, kv, p_s, dp_s, ds_s, m_s, l_s, w_s, own_part,
    gy_out, gy_in, gz_out, gz_in,
    in_sem, kvz_send, kvz_recv, kvy_send, kvy_recv,
    gy_send, gy_recv, gz_send, gz_recv,
):
    chain = n // 2
    place = lax.axis_index("ctx")
    head = lax.axis_index("head")
    a, b = place // 2, lax.rem(place, 2)
    rows_flat = q_ref.shape[0]
    rows = rows_flat // GROUP
    part = rows // heads
    scale = 1.0 / math.sqrt(DH)
    power = scale * math.log2(math.e)
    chunk = min(ROW_CHUNK, rows_flat)
    chunks = [slice(r, r + chunk) for r in range(0, rows_flat, chunk)]

    def head_peer(d):
        return lax.rem(head + d, heads)

    def up(d):
        return lax.rem(a + d, chain)

    def down(d):
        return lax.rem(a + chain - d, chain)

    def at(ctx_index, head_index):
        return (ctx_index, head_index)

    partner = 2 * a + 1 - b

    def send(src, dst, send_sem, recv_sem, target):
        return pltpu.make_async_remote_copy(
            src_ref=src, dst_ref=dst, send_sem=send_sem, recv_sem=recv_sem,
            device_id=target, device_id_type=MESH,
        )

    pairs = [(da, dh) for da in range(chain) for dh in range(heads)]
    others = pairs[1:]

    barrier = pltpu.get_barrier_semaphore()
    for da, dh in others:
        pl.semaphore_signal(
            barrier, inc=1, device_id=at(2 * up(da) + b, head_peer(dh)), device_id_type=MESH
        )
    pl.semaphore_signal(barrier, inc=1, device_id=at(partner, head), device_id_type=MESH)

    loads = [
        pltpu.make_async_copy(src, dst, in_sem.at[i])
        for i, (src, dst) in enumerate((
            (k_hbm, k_ref), (v_hbm, v_ref), (blocks_hbm, blocks_ref),
            (audio_hbm, audio_ref), (q_hbm, q_ref), (do_hbm, do_ref),
        ))
    ]
    for load in loads:
        load.start()
    loads[0].wait()
    loads[1].wait()
    for i in range(heads):
        head_out[i, 0] = k_ref[:, i, :]
        head_out[i, 1] = v_ref[:, i, :]
    pl.semaphore_wait(barrier, chain * heads)

    mine = pl.ds(pl.multiple_of(head * part, part), part)

    def chain_copy(da, dh):
        peer = head_peer(dh)
        return send(
            head_out.at[peer], kv.at[place, :, mine, :], kvz_send.at[da * heads + dh],
            kvz_recv.at[a * heads + head], at(2 * up(da) + b, peer),
        )

    def chain_arrival(d, dh):
        source, peer = down(d), head_peer(dh)
        theirs = pl.ds(pl.multiple_of(peer * part, part), part)
        return send(
            head_out.at[peer], kv.at[2 * source + b, :, theirs, :], kvz_send.at[0],
            kvz_recv.at[source * heads + peer], at(partner, head),
        )

    def relay_copy(d):
        slot = 2 * down(d) + b
        return send(kv.at[slot], kv.at[slot], kvy_send.at[d], kvy_recv.at[down(d)], at(partner, head))

    def relay_arrival(d):
        slot = 2 * down(d) + 1 - b
        return send(kv.at[slot], kv.at[slot], kvy_send.at[d], kvy_recv.at[down(d)], at(partner, head))

    for da, dh in others:
        chain_copy(da, dh).start()
    kv[place, :, mine, :] = head_out[head]

    for load in loads[2:]:
        load.wait()
    q_turned[...] = q_ref[...].T
    do_turned[...] = do_ref[...].T

    pos = place * rows + lax.broadcasted_iota(jnp.int32, (1, rows_flat), 1) // GROUP
    limit = pos + 1
    start = jnp.int32(0)
    for s in range(blocks_ref.shape[0]):
        end = start + blocks_ref[s] * BLK
        inside = (pos >= start) & (pos < end) & (jnp.broadcast_to(audio_ref[s], pos.shape) == 1)
        limit = jnp.where(inside, end, limit)
        start = end

    for dh in range(1, heads):
        chain_arrival(0, dh).wait_recv()
    relay_copy(0).start()

    def stats_step(t, carry):
        d = t // 2
        own_column = lax.rem(t, 2) == 0
        slot = 2 * down(d) + lax.rem(b + t, 2)

        @pl.when(own_column & (t > 0))
        def _():
            for dh in range(heads):
                chain_arrival(d, dh).wait_recv()
            relay_copy(d).start()

        @pl.when(jnp.logical_not(own_column))
        def _():
            relay_arrival(d).wait_recv()

        keys, values = kv[slot, 0], kv[slot, 1]
        key_pos = slot * rows + lax.broadcasted_iota(jnp.int32, (rows, 1), 0)
        for c in chunks:
            s = jnp.dot(keys, q_turned[:, c], preferred_element_type=jnp.float32)
            s = jnp.where(key_pos < limit[:, c], s, NEG)
            high = jnp.max(s, axis=0, keepdims=True)
            p = jnp.exp2((s - high) * power)
            dp = jnp.dot(values, do_turned[:, c], preferred_element_type=jnp.float32)
            p_s[slot, :, c] = p
            dp_s[slot, :, c] = dp
            m_s[slot, :, c] = high
            l_s[slot, :, c] = jnp.sum(p, axis=0, keepdims=True)
            w_s[slot, :, c] = jnp.sum(p * dp, axis=0, keepdims=True)
        return carry

    lax.fori_loop(0, n, stats_step, 0)

    m_all = m_s[...]
    high = jnp.max(m_all, axis=0)
    factors = jnp.exp2((m_all - high[None]) * power)
    total = jnp.sum(factors * l_s[...], axis=0)
    delta = jnp.sum(factors * w_s[...], axis=0) / total
    m_s[...] = factors / total[None]

    def pair_copy(d):
        dest = down(d)
        return send(gy_out.at[d], gy_in.at[dest], gy_send.at[d], gy_recv.at[dest], at(partner, head))

    def sum_copy(d, dh):
        peer = head_peer(dh)
        theirs = pl.ds(pl.multiple_of(peer * part, part), part)
        return send(
            gz_out.at[d, :, theirs, :], gz_in.at[a * heads + head], gz_send.at[d * heads + dh],
            gz_recv.at[a * heads + head], at(2 * down(d) + b, peer),
        )

    def sum_arrival(da, dh):
        index = up(da) * heads + head_peer(dh)
        return send(
            gz_out.at[0, :, mine, :], gz_in.at[index], gz_send.at[0], gz_recv.at[index], at(partner, head)
        )

    def combine(d):
        pair_copy(d).wait_recv()
        return own_part[d] + gy_in[down(d)].astype(jnp.float32)

    def grad_step(t, carry):
        d = lax.rem(t // 2 + 1, chain)
        other_column = lax.rem(t, 2) == 0
        slot = 2 * down(d) + lax.rem(b + t + 1, 2)
        key_part = jnp.zeros((rows, DH), jnp.float32)
        value_part = jnp.zeros((rows, DH), jnp.float32)
        for c in chunks:
            probs = p_s[slot, :, c] * m_s[slot, :, c]
            ds = (probs * (dp_s[slot, :, c] - delta[:, c])).astype(jnp.bfloat16)
            ds_s[slot, :, c] = ds
            value_part += jnp.dot(probs.astype(jnp.bfloat16), do_ref[c, :], preferred_element_type=jnp.float32)
            key_part += jnp.dot(ds, q_ref[c, :], preferred_element_type=jnp.float32)

        @pl.when(other_column)
        def _():
            gy_out[d, 0] = key_part.astype(jnp.bfloat16)
            gy_out[d, 1] = value_part.astype(jnp.bfloat16)
            pair_copy(d).start()

        @pl.when(jnp.logical_not(other_column))
        def _():
            own_part[d, 0] = key_part
            own_part[d, 1] = value_part

        @pl.when(jnp.logical_not(other_column) & (t > 1))
        def _():
            before = t // 2
            gz_out[before] = combine(before).astype(jnp.bfloat16)
            for dh in range(heads):
                sum_copy(before, dh).start()

        return carry

    lax.fori_loop(0, n, grad_step, 0)

    all_keys = kv[:, 0].reshape(n * rows, DH)

    def query_rows(c):
        all_ds = ds_s[:, :, c].reshape(n * rows, c.stop - c.start)
        dq_ref[c, :] = (contract_first(all_keys, all_ds) * scale).T.astype(jnp.bfloat16)

    middle = rows_flat // 2
    query_rows(slice(0, middle))
    gz_out[0] = combine(0).astype(jnp.bfloat16)
    for dh in range(1, heads):
        sum_copy(0, dh).start()
    gz_in[a * heads + head] = gz_out[0, :, mine, :]
    query_rows(slice(middle, rows_flat))

    for da, dh in others:
        sum_arrival(da, dh).wait_recv()
    for i in range(heads):
        acc = gz_in[i].astype(jnp.float32)
        for source in range(1, chain):
            acc = acc + gz_in[source * heads + i].astype(jnp.float32)
        dk_ref[:, i, :] = (acc[0] * scale).astype(jnp.bfloat16)
        dv_ref[:, i, :] = acc[1].astype(jnp.bfloat16)

    for da, dh in others:
        chain_copy(da, dh).wait_send()
        sum_copy(da, dh).wait_send()
    for d in range(chain):
        relay_copy(d).wait_send()
        pair_copy(d).wait_send()


def fused_scratch(n, heads, rows, segments):
    flat, chain, part = rows * GROUP, n // 2, rows // heads
    low, full, sem = jnp.bfloat16, jnp.float32, pltpu.SemaphoreType.DMA
    return [
        pltpu.VMEM((flat, DH), low),
        pltpu.VMEM((flat, DH), low),
        pltpu.VMEM((part, heads, DH), low),
        pltpu.VMEM((part, heads, DH), low),
        pltpu.SMEM((segments,), jnp.int32),
        pltpu.SMEM((segments,), jnp.int32),
        pltpu.VMEM((DH, flat), low),
        pltpu.VMEM((DH, flat), low),
        pltpu.VMEM((heads, 2, part, DH), low),
        pltpu.VMEM((n, 2, rows, DH), low),
        pltpu.VMEM((n, rows, flat), full),
        pltpu.VMEM((n, rows, flat), full),
        pltpu.VMEM((n, rows, flat), low),
        pltpu.VMEM((n, 1, flat), full),
        pltpu.VMEM((n, 1, flat), full),
        pltpu.VMEM((n, 1, flat), full),
        pltpu.VMEM((chain, 2, rows, DH), full),
        pltpu.VMEM((chain, 2, rows, DH), low),
        pltpu.VMEM((chain, 2, rows, DH), low),
        pltpu.VMEM((chain, 2, rows, DH), low),
        pltpu.VMEM((chain * heads, 2, part, DH), low),
        sem((6,)), sem((chain * heads,)), sem((chain * heads,)), sem((chain,)), sem((chain,)),
        sem((chain,)), sem((chain,)), sem((chain * heads,)), sem((chain * heads,)),
    ]


def fused_body(n, heads, query, key, value, d_out, seg_blocks, seg_audio):
    rows = query.shape[0]
    flat = rows * GROUP
    low = jnp.bfloat16
    vmem, hbm = pl.BlockSpec(memory_space=pltpu.VMEM), pl.BlockSpec(memory_space=pltpu.HBM)
    d_query, d_key, d_value = pl.pallas_call(
        functools.partial(fused_kernel, n, heads),
        out_shape=[
            jax.ShapeDtypeStruct((flat, DH), low),
            jax.ShapeDtypeStruct(key.shape, low),
            jax.ShapeDtypeStruct(value.shape, low),
        ],
        in_specs=[hbm] * 6,
        out_specs=[vmem] * 3,
        scratch_shapes=fused_scratch(n, heads, rows, seg_blocks.shape[0]),
        cost_estimate=pl.CostEstimate(
            flops=10 * n * rows * flat * DH, bytes_accessed=6 * flat * DH, transcendentals=n * rows * flat
        ),
        compiler_params=pltpu.CompilerParams(
            collective_id=0, has_side_effects=True, vmem_limit_bytes=VMEM_BUDGET
        ),
    )(query.reshape(flat, DH), d_out.reshape(flat, DH), key, value, seg_blocks, seg_audio)
    return d_query.reshape(query.shape), d_key, d_value


def plan_body(n, heads, query, key, value, d_out, seg_blocks, seg_audio):
    rows = query.shape[0]
    held = n * rows * rows * GROUP * 10
    if held > VMEM_BUDGET // 2 or n % 2 or query.shape[1] != GROUP or key.shape[1] != heads:
        return body(query, key, value, d_out, seg_blocks, seg_audio)
    return fused_body(n, heads, query, key, value, d_out, seg_blocks, seg_audio)


def solution(mesh):
    placed = (
        P("ctx", "head", None),
        P(("ctx", "head"), None, None),
        P(("ctx", "head"), None, None),
        P("ctx", "head", None),
        P(),
        P(),
    )
    return jax.shard_map(
        functools.partial(plan_body, mesh.shape["ctx"], mesh.shape["head"]),
        mesh=mesh,
        in_specs=placed,
        out_specs=(
            P("ctx", "head", None),
            P(("ctx", "head"), None, None),
            P(("ctx", "head"), None, None),
        ),
        check_vma=False,
    )
```

```python
import functools
import math

import jax
import jax.numpy as jnp
from jax import lax
from jax.experimental import pallas as pl
from jax.experimental.pallas import tpu as pltpu
from jax.sharding import PartitionSpec as P

MESH = pl.DeviceIdType.MESH
VMEM_BUDGET = 60 * 2**20
ROW_CHUNK = 256
OUTER = 2.0**-4

DH = 128
GROUP = 8
BLK = 128


NEG = -1e30


def segment_tables(seg_blocks, seg_audio, positions):
    ends = jnp.cumsum(seg_blocks)
    starts = ends - seg_blocks
    blocks = positions // BLK
    inside = (starts[None, :] <= blocks[:, None]) & (blocks[:, None] < ends[None, :])
    numbers = jnp.arange(seg_blocks.shape[0], dtype=jnp.int32)
    segment = jnp.sum(jnp.where(inside, numbers[None, :], 0), axis=1)
    audio = jnp.sum(jnp.where(inside, seg_audio[None, :], 0), axis=1)
    return (segment, audio)


def visible(query_pos, key_pos, query_seg, query_audio, key_seg):
    causal = key_pos[None, :] <= query_pos[:, None]
    span = (query_seg[:, None] == key_seg[None, :]) & (query_audio[:, None] == 1)
    return causal | span


def prepare(rows_query, rows_out, query_pos, seg_blocks, seg_audio):
    tokens = rows_query.shape[0]
    query_seg, query_audio = segment_tables(seg_blocks, seg_audio, query_pos)
    query_flat = rows_query.reshape(tokens * GROUP, DH)
    out_flat = rows_out.reshape(tokens * GROUP, DH)
    return (query_flat, out_flat, query_pos, query_seg, query_audio)


def piece_mask(group_data, keys, seg_blocks, seg_audio):
    query_flat, out_flat, query_pos, query_seg, query_audio = group_data
    key_pos = jnp.arange(keys.shape[0], dtype=jnp.int32)
    key_seg = segment_tables(seg_blocks, seg_audio, key_pos)[0]
    return visible(query_pos, key_pos, query_seg, query_audio, key_seg)


def contract_rows(left, right):
    return lax.dot_general(
        left, right, (((1,), (1,)), ((), ())), preferred_element_type=jnp.float32
    )


def contract_first(left, right):
    return lax.dot_general(
        left, right, (((0,), (0,)), ((), ())), preferred_element_type=jnp.float32
    )


def stats_group(group_data, state, piece, seg_blocks, seg_audio):
    query_flat, out_flat, query_pos, query_seg, query_audio = group_data
    keys, values = piece
    count = keys.shape[0]
    tokens = query_pos.shape[0]
    scale = 1.0 / math.sqrt(DH)
    mask = piece_mask(group_data, keys, seg_blocks, seg_audio)

    def stats_compute(kept):
        highest, total, weighted = kept
        wide = mask[:, None, :]
        scores = (contract_rows(query_flat, keys) * scale).reshape(tokens, GROUP, count)
        new_high = jnp.maximum(highest, jnp.max(jnp.where(wide, scores, NEG), axis=2))
        probs = jnp.where(wide, jnp.exp(scores - new_high[:, :, None]), 0.0)
        d_probs = contract_rows(out_flat, values).reshape(tokens, GROUP, count)
        return (new_high, jnp.sum(probs, axis=2), jnp.sum(probs * d_probs, axis=2))

    def stats_skipped(kept):
        return kept

    return lax.cond(jnp.any(mask), stats_compute, stats_skipped, state)


def grad_group(group_data, finals, grad_rows, piece, seg_blocks, seg_audio):
    query_flat, out_flat, query_pos, query_seg, query_audio = group_data
    lse, delta = finals
    keys, values = piece
    count = keys.shape[0]
    tokens = query_pos.shape[0]
    scale = 1.0 / math.sqrt(DH)
    mask = piece_mask(group_data, keys, seg_blocks, seg_audio)

    def grad_compute(grad_rows):
        wide = mask[:, None, :]
        scores = (contract_rows(query_flat, keys) * scale).reshape(tokens, GROUP, count)
        probs = jnp.where(wide, jnp.exp(scores - lse[:, :, None]), 0.0)
        d_probs = contract_rows(out_flat, values).reshape(tokens, GROUP, count)
        probs_low = probs.astype(jnp.bfloat16).reshape(tokens * GROUP, count)
        d_scores = (
            (probs * (d_probs - delta[:, :, None]))
            .astype(jnp.bfloat16)
            .reshape(tokens * GROUP, count)
        )
        value_part = contract_first(probs_low, out_flat)
        key_part = contract_first(d_scores, query_flat)
        grad_rows = jnp.dot(d_scores, keys, preferred_element_type=jnp.float32)
        return (grad_rows, key_part, value_part)

    def grad_skipped(grad_rows):
        blank = jnp.zeros((count, keys.shape[1]), jnp.float32)
        return (grad_rows, blank, blank)

    return lax.cond(jnp.any(mask), grad_compute, grad_skipped, grad_rows)


def body(query, key, value, d_out, seg_blocks, seg_audio):
    key, value = (
        lax.all_to_all(key, "head", split_axis=1, concat_axis=0, tiled=True),
        lax.all_to_all(value, "head", split_axis=1, concat_axis=0, tiled=True),
    )
    rows = query.shape[0]
    half = rows // 2
    place = lax.axis_index("ctx")
    scale = 1.0 / math.sqrt(DH)
    keys = key[:, 0, :]
    values = value[:, 0, :]
    own_pos = place * rows + jnp.arange(rows, dtype=jnp.int32)
    first = prepare(query[:half], d_out[:half], own_pos[:half], seg_blocks, seg_audio)
    second = prepare(query[half:], d_out[half:], own_pos[half:], seg_blocks, seg_audio)
    groups = (first, second)
    blank_stats = jnp.zeros((half, GROUP), jnp.float32)
    start_stats = tuple(
        (
            (jnp.full((half, GROUP), NEG, jnp.float32), blank_stats, blank_stats)
            for group_data in groups
        )
    )
    piece = (
        lax.all_gather(keys, "ctx", axis=0, tiled=True),
        lax.all_gather(values, "ctx", axis=0, tiled=True),
    )
    stats = tuple(
        (
            stats_group(group_data, state, piece, seg_blocks, seg_audio)
            for group_data, state in zip(groups, start_stats)
        )
    )
    finals = tuple(
        ((highest + jnp.log(total), weighted / total) for highest, total, weighted in stats)
    )
    blank_rows = jnp.zeros((half * GROUP, DH), jnp.float32)
    piece = (
        lax.all_gather(keys, "ctx", axis=0, tiled=True),
        lax.all_gather(values, "ctx", axis=0, tiled=True),
    )
    grad_list = (blank_rows, blank_rows)
    piece_keys = piece[0]
    count = piece_keys.shape[0]
    key_sum = jnp.zeros((count, DH), jnp.float32)
    value_sum = jnp.zeros((count, DH), jnp.float32)
    new_rows = []
    for group_data, group_finals, grad_rows in zip(groups, finals, grad_list):
        grad_rows, key_part, value_part = grad_group(
            group_data, group_finals, grad_rows, piece, seg_blocks, seg_audio
        )
        key_sum = key_sum + key_part
        value_sum = value_sum + value_part
        new_rows.append(grad_rows)
    update = jnp.stack([key_sum, value_sum], axis=1)
    key_grad = update
    grads = (key_grad, tuple(new_rows))
    key_grad, grad_list = grads
    summed = lax.psum_scatter(key_grad, "ctx", scatter_dimension=0, tiled=True)
    d_key = (summed[:, 0, :] * scale).astype(jnp.bfloat16)[:, None, :]
    d_value = summed[:, 1, :].astype(jnp.bfloat16)[:, None, :]
    first_rows = (grad_list[0] * scale).astype(jnp.bfloat16).reshape(half, GROUP, DH)
    second_rows = (grad_list[1] * scale).astype(jnp.bfloat16).reshape(half, GROUP, DH)
    d_query = jnp.concatenate([first_rows, second_rows], axis=0)
    d_key, d_value = (
        lax.all_to_all(d_key, "head", split_axis=0, concat_axis=1, tiled=True),
        lax.all_to_all(d_value, "head", split_axis=0, concat_axis=1, tiled=True),
    )
    return (d_query, d_key, d_value)


def fused_kernel(
    n, heads, q_hbm, do_hbm, k_hbm, v_hbm, blocks_hbm, audio_hbm,
    dq_ref, dk_ref, dv_ref,
    q_ref, do_ref, k_ref, v_ref, blocks_ref, audio_ref, q_turned, do_turned,
    head_out, kv, p_s, dp_s, ds_s, m_s, l_s, w_s, own_part,
    gy_out, gy_in, gz_out, gz_in,
    in_sem, kvz_send, kvz_recv, kvy_send, kvy_recv,
    gy_send, gy_recv, gz_send, gz_recv,
):
    chain = n // 2
    place = lax.axis_index("ctx")
    head = lax.axis_index("head")
    a, b = place // 2, lax.rem(place, 2)
    rows_flat = q_ref.shape[0]
    rows = rows_flat // GROUP
    part = rows // heads
    scale = 1.0 / math.sqrt(DH)
    power = scale * math.log2(math.e)
    inner = scale / OUTER
    chunk = min(ROW_CHUNK, rows_flat)
    chunks = [slice(r, r + chunk) for r in range(0, rows_flat, chunk)]

    def head_peer(d):
        return lax.rem(head + d, heads)

    def up(d):
        return lax.rem(a + d, chain)

    def down(d):
        return lax.rem(a + chain - d, chain)

    def at(ctx_index, head_index):
        return (ctx_index, head_index)

    partner = 2 * a + 1 - b

    def send(src, dst, send_sem, recv_sem, target):
        return pltpu.make_async_remote_copy(
            src_ref=src, dst_ref=dst, send_sem=send_sem, recv_sem=recv_sem,
            device_id=target, device_id_type=MESH,
        )

    pairs = [(da, dh) for da in range(chain) for dh in range(heads)]
    others = pairs[1:]

    barrier = pltpu.get_barrier_semaphore()
    for da, dh in others:
        pl.semaphore_signal(
            barrier, inc=1, device_id=at(2 * up(da) + b, head_peer(dh)), device_id_type=MESH
        )
    pl.semaphore_signal(barrier, inc=1, device_id=at(partner, head), device_id_type=MESH)

    loads = [
        pltpu.make_async_copy(src, dst, in_sem.at[i])
        for i, (src, dst) in enumerate((
            (k_hbm, k_ref), (v_hbm, v_ref), (blocks_hbm, blocks_ref),
            (audio_hbm, audio_ref), (q_hbm, q_ref), (do_hbm, do_ref),
        ))
    ]
    for load in loads:
        load.start()
    loads[0].wait()
    loads[1].wait()
    for i in range(heads):
        head_out[i, 0] = k_ref[:, i, :]
        head_out[i, 1] = v_ref[:, i, :]
    pl.semaphore_wait(barrier, chain * heads)

    mine = pl.ds(pl.multiple_of(head * part, part), part)

    def chain_copy(da, dh):
        peer = head_peer(dh)
        return send(
            head_out.at[peer], kv.at[place, :, mine, :], kvz_send.at[da * heads + dh],
            kvz_recv.at[a * heads + head], at(2 * up(da) + b, peer),
        )

    def chain_arrival(d, dh):
        source, peer = down(d), head_peer(dh)
        theirs = pl.ds(pl.multiple_of(peer * part, part), part)
        return send(
            head_out.at[peer], kv.at[2 * source + b, :, theirs, :], kvz_send.at[0],
            kvz_recv.at[source * heads + peer], at(partner, head),
        )

    def relay_copy(d):
        slot = 2 * down(d) + b
        return send(kv.at[slot], kv.at[slot], kvy_send.at[d], kvy_recv.at[down(d)], at(partner, head))

    def relay_arrival(d):
        slot = 2 * down(d) + 1 - b
        return send(kv.at[slot], kv.at[slot], kvy_send.at[d], kvy_recv.at[down(d)], at(partner, head))

    for da, dh in others:
        chain_copy(da, dh).start()
    kv[place, :, mine, :] = head_out[head]

    for load in loads[2:]:
        load.wait()
    q_turned[...] = q_ref[...].T
    do_turned[...] = do_ref[...].T

    pos = place * rows + lax.broadcasted_iota(jnp.int32, (1, rows_flat), 1) // GROUP
    limit = pos + 1
    start = jnp.int32(0)
    for s in range(blocks_ref.shape[0]):
        end = start + blocks_ref[s] * BLK
        inside = (pos >= start) & (pos < end) & (jnp.broadcast_to(audio_ref[s], pos.shape) == 1)
        limit = jnp.where(inside, end, limit)
        start = end

    for dh in range(1, heads):
        chain_arrival(0, dh).wait_recv()
    relay_copy(0).start()

    key_pos = lax.broadcasted_iota(jnp.int32, (rows, 1), 0)

    def stats_step(t, carry):
        d = t // 2
        own_column = lax.rem(t, 2) == 0
        slot = 2 * down(d) + lax.rem(b + t, 2)

        @pl.when(own_column & (t > 0))
        def _():
            for dh in range(heads):
                chain_arrival(d, dh).wait_recv()
            relay_copy(d).start()

        @pl.when(jnp.logical_not(own_column))
        def _():
            relay_arrival(d).wait_recv()

        keys, values = kv[slot, 0], kv[slot, 1]
        s_all = jnp.dot(keys, q_turned[...], preferred_element_type=jnp.float32)
        dp_all = jnp.dot(values, do_turned[...], preferred_element_type=jnp.float32)
        bound = limit - slot * rows
        found = []
        for c in chunks:
            s = jnp.where(key_pos < bound[:, c], s_all[:, c], NEG)
            high = jnp.max(s, axis=0, keepdims=True)
            p = jnp.exp2((s - high) * power)
            total = jnp.sum(p, axis=0, keepdims=True)
            weighted = jnp.sum(p * dp_all[:, c], axis=0, keepdims=True)
            found.append((p, high, total, weighted))
        dp_s[slot] = dp_all
        for c, (p, high, total, weighted) in zip(chunks, found):
            p_s[slot, :, c] = p
            m_s[slot, :, c] = high
            l_s[slot, :, c] = total
            w_s[slot, :, c] = weighted
        return carry

    lax.fori_loop(0, n, stats_step, 0)

    m_all = m_s[...]
    high = jnp.max(m_all, axis=0)
    factors = jnp.exp2((m_all - high[None]) * power)
    total = jnp.sum(factors * l_s[...], axis=0)
    delta = jnp.sum(factors * w_s[...], axis=0) / total
    m_s[...] = factors / total[None]

    def pair_copy(d):
        dest = down(d)
        return send(gy_out.at[d], gy_in.at[dest], gy_send.at[d], gy_recv.at[dest], at(partner, head))

    def sum_copy(d, dh):
        peer = head_peer(dh)
        theirs = pl.ds(pl.multiple_of(peer * part, part), part)
        return send(
            gz_out.at[d, :, theirs, :], gz_in.at[a * heads + head], gz_send.at[d * heads + dh],
            gz_recv.at[a * heads + head], at(2 * down(d) + b, peer),
        )

    def sum_arrival(da, dh):
        index = up(da) * heads + head_peer(dh)
        return send(
            gz_out.at[0, :, mine, :], gz_in.at[index], gz_send.at[0], gz_recv.at[index], at(partner, head)
        )

    def combine(d):
        pair_copy(d).wait_recv()
        return own_part[d] + gy_in[down(d)].astype(jnp.float32)

    def grad_step(t, carry):
        d = lax.rem(t // 2 + 1, chain)
        other_column = lax.rem(t, 2) == 0
        slot = 2 * down(d) + lax.rem(b + t + 1, 2)
        probs_low, ds = [], []
        for c in chunks:
            probs = p_s[slot, :, c] * m_s[slot, :, c]
            probs_low.append(probs.astype(jnp.bfloat16))
            ds.append((probs * (dp_s[slot, :, c] - delta[:, c])).astype(jnp.bfloat16))
        probs_low, ds = jnp.concatenate(probs_low, axis=1), jnp.concatenate(ds, axis=1)
        value_part = jnp.dot(probs_low, do_ref[...], preferred_element_type=jnp.float32)
        key_part = jnp.dot(ds, q_ref[...], preferred_element_type=jnp.float32)
        ds_s[slot] = ds

        @pl.when(other_column)
        def _():
            gy_out[d, 0] = key_part.astype(jnp.bfloat16)
            gy_out[d, 1] = value_part.astype(jnp.bfloat16)
            pair_copy(d).start()

        @pl.when(jnp.logical_not(other_column))
        def _():
            own_part[d, 0] = key_part
            own_part[d, 1] = value_part

        @pl.when(jnp.logical_not(other_column) & (t > 1))
        def _():
            before = t // 2
            gz_out[before] = combine(before).astype(jnp.bfloat16)
            for dh in range(heads):
                sum_copy(before, dh).start()

        return carry

    lax.fori_loop(0, n, grad_step, 0)

    all_keys = kv[:, 0].reshape(n * rows, DH)

    def query_rows(c):
        all_ds = ds_s[:, :, c].reshape(n * rows, c.stop - c.start)
        dq_ref[c, :] = (contract_first(all_keys, all_ds) * inner).T.astype(jnp.bfloat16)

    middle = rows_flat // 2
    query_rows(slice(0, middle))
    gz_out[0] = combine(0).astype(jnp.bfloat16)
    for dh in range(1, heads):
        sum_copy(0, dh).start()
    gz_in[a * heads + head] = gz_out[0, :, mine, :]
    query_rows(slice(middle, rows_flat))

    for da, dh in others:
        sum_arrival(da, dh).wait_recv()
    for i in range(heads):
        acc = gz_in[i].astype(jnp.float32)
        for source in range(1, chain):
            acc = acc + gz_in[source * heads + i].astype(jnp.float32)
        dk_ref[:, i, :] = (acc[0] * inner).astype(jnp.bfloat16)
        dv_ref[:, i, :] = (acc[1] / OUTER).astype(jnp.bfloat16)

    for da, dh in others:
        chain_copy(da, dh).wait_send()
        sum_copy(da, dh).wait_send()
    for d in range(chain):
        relay_copy(d).wait_send()
        pair_copy(d).wait_send()


def fused_scratch(n, heads, rows, segments):
    flat, chain, part = rows * GROUP, n // 2, rows // heads
    low, full, sem = jnp.bfloat16, jnp.float32, pltpu.SemaphoreType.DMA
    return [
        pltpu.VMEM((flat, DH), low),
        pltpu.VMEM((flat, DH), low),
        pltpu.VMEM((part, heads, DH), low),
        pltpu.VMEM((part, heads, DH), low),
        pltpu.SMEM((segments,), jnp.int32),
        pltpu.SMEM((segments,), jnp.int32),
        pltpu.VMEM((DH, flat), low),
        pltpu.VMEM((DH, flat), low),
        pltpu.VMEM((heads, 2, part, DH), low),
        pltpu.VMEM((n, 2, rows, DH), low),
        pltpu.VMEM((n, rows, flat), full),
        pltpu.VMEM((n, rows, flat), full),
        pltpu.VMEM((n, rows, flat), low),
        pltpu.VMEM((n, 1, flat), full),
        pltpu.VMEM((n, 1, flat), full),
        pltpu.VMEM((n, 1, flat), full),
        pltpu.VMEM((chain, 2, rows, DH), full),
        pltpu.VMEM((chain, 2, rows, DH), low),
        pltpu.VMEM((chain, 2, rows, DH), low),
        pltpu.VMEM((chain, 2, rows, DH), low),
        pltpu.VMEM((chain * heads, 2, part, DH), low),
        sem((6,)), sem((chain * heads,)), sem((chain * heads,)), sem((chain,)), sem((chain,)),
        sem((chain,)), sem((chain,)), sem((chain * heads,)), sem((chain * heads,)),
    ]


def fused_body(n, heads, query, key, value, d_out, seg_blocks, seg_audio):
    rows = query.shape[0]
    flat = rows * GROUP
    low = jnp.bfloat16
    vmem, hbm = pl.BlockSpec(memory_space=pltpu.VMEM), pl.BlockSpec(memory_space=pltpu.HBM)
    d_query, d_key, d_value = pl.pallas_call(
        functools.partial(fused_kernel, n, heads),
        out_shape=[
            jax.ShapeDtypeStruct((flat, DH), low),
            jax.ShapeDtypeStruct(key.shape, low),
            jax.ShapeDtypeStruct(value.shape, low),
        ],
        in_specs=[hbm] * 6,
        out_specs=[vmem] * 3,
        scratch_shapes=fused_scratch(n, heads, rows, seg_blocks.shape[0]),
        cost_estimate=pl.CostEstimate(
            flops=10 * n * rows * flat * DH, bytes_accessed=6 * flat * DH, transcendentals=n * rows * flat
        ),
        compiler_params=pltpu.CompilerParams(
            collective_id=0, has_side_effects=True, vmem_limit_bytes=VMEM_BUDGET
        ),
    )(query.reshape(flat, DH), d_out.reshape(flat, DH), key, value, seg_blocks, seg_audio)
    d_query = d_query.reshape(query.shape)
    return tuple(grad * jnp.asarray(OUTER, low) for grad in (d_query, d_key, d_value))


def plan_body(n, heads, query, key, value, d_out, seg_blocks, seg_audio):
    rows = query.shape[0]
    held = n * rows * rows * GROUP * 10
    if held > VMEM_BUDGET // 2 or n % 2 or query.shape[1] != GROUP or key.shape[1] != heads:
        return body(query, key, value, d_out, seg_blocks, seg_audio)
    return fused_body(n, heads, query, key, value, d_out, seg_blocks, seg_audio)


def solution(mesh):
    placed = (
        P("ctx", "head", None),
        P(("ctx", "head"), None, None),
        P(("ctx", "head"), None, None),
        P("ctx", "head", None),
        P(),
        P(),
    )
    return jax.shard_map(
        functools.partial(plan_body, mesh.shape["ctx"], mesh.shape["head"]),
        mesh=mesh,
        in_specs=placed,
        out_specs=(
            P("ctx", "head", None),
            P(("ctx", "head"), None, None),
            P(("ctx", "head"), None, None),
        ),
        check_vma=False,
    )
```

```python
import functools
import math

import jax
import jax.numpy as jnp
from jax import lax
from jax.experimental import pallas as pl
from jax.experimental.pallas import tpu as pltpu
from jax.sharding import PartitionSpec as P

MESH = pl.DeviceIdType.MESH
VMEM_BUDGET = 60 * 2**20
ROW_CHUNK = 256
OUTER = 2.0**-4

DH = 128
GROUP = 8
BLK = 128


NEG = -1e30


def segment_tables(seg_blocks, seg_audio, positions):
    ends = jnp.cumsum(seg_blocks)
    starts = ends - seg_blocks
    blocks = positions // BLK
    inside = (starts[None, :] <= blocks[:, None]) & (blocks[:, None] < ends[None, :])
    numbers = jnp.arange(seg_blocks.shape[0], dtype=jnp.int32)
    segment = jnp.sum(jnp.where(inside, numbers[None, :], 0), axis=1)
    audio = jnp.sum(jnp.where(inside, seg_audio[None, :], 0), axis=1)
    return (segment, audio)


def visible(query_pos, key_pos, query_seg, query_audio, key_seg):
    causal = key_pos[None, :] <= query_pos[:, None]
    span = (query_seg[:, None] == key_seg[None, :]) & (query_audio[:, None] == 1)
    return causal | span


def prepare(rows_query, rows_out, query_pos, seg_blocks, seg_audio):
    tokens = rows_query.shape[0]
    query_seg, query_audio = segment_tables(seg_blocks, seg_audio, query_pos)
    query_flat = rows_query.reshape(tokens * GROUP, DH)
    out_flat = rows_out.reshape(tokens * GROUP, DH)
    return (query_flat, out_flat, query_pos, query_seg, query_audio)


def piece_mask(group_data, keys, seg_blocks, seg_audio):
    query_flat, out_flat, query_pos, query_seg, query_audio = group_data
    key_pos = jnp.arange(keys.shape[0], dtype=jnp.int32)
    key_seg = segment_tables(seg_blocks, seg_audio, key_pos)[0]
    return visible(query_pos, key_pos, query_seg, query_audio, key_seg)


def contract_rows(left, right):
    return lax.dot_general(
        left, right, (((1,), (1,)), ((), ())), preferred_element_type=jnp.float32
    )


def contract_first(left, right):
    return lax.dot_general(
        left, right, (((0,), (0,)), ((), ())), preferred_element_type=jnp.float32
    )


def stats_group(group_data, state, piece, seg_blocks, seg_audio):
    query_flat, out_flat, query_pos, query_seg, query_audio = group_data
    keys, values = piece
    count = keys.shape[0]
    tokens = query_pos.shape[0]
    scale = 1.0 / math.sqrt(DH)
    mask = piece_mask(group_data, keys, seg_blocks, seg_audio)

    def stats_compute(kept):
        highest, total, weighted = kept
        wide = mask[:, None, :]
        scores = (contract_rows(query_flat, keys) * scale).reshape(tokens, GROUP, count)
        new_high = jnp.maximum(highest, jnp.max(jnp.where(wide, scores, NEG), axis=2))
        probs = jnp.where(wide, jnp.exp(scores - new_high[:, :, None]), 0.0)
        d_probs = contract_rows(out_flat, values).reshape(tokens, GROUP, count)
        return (new_high, jnp.sum(probs, axis=2), jnp.sum(probs * d_probs, axis=2))

    def stats_skipped(kept):
        return kept

    return lax.cond(jnp.any(mask), stats_compute, stats_skipped, state)


def grad_group(group_data, finals, grad_rows, piece, seg_blocks, seg_audio):
    query_flat, out_flat, query_pos, query_seg, query_audio = group_data
    lse, delta = finals
    keys, values = piece
    count = keys.shape[0]
    tokens = query_pos.shape[0]
    scale = 1.0 / math.sqrt(DH)
    mask = piece_mask(group_data, keys, seg_blocks, seg_audio)

    def grad_compute(grad_rows):
        wide = mask[:, None, :]
        scores = (contract_rows(query_flat, keys) * scale).reshape(tokens, GROUP, count)
        probs = jnp.where(wide, jnp.exp(scores - lse[:, :, None]), 0.0)
        d_probs = contract_rows(out_flat, values).reshape(tokens, GROUP, count)
        probs_low = probs.astype(jnp.bfloat16).reshape(tokens * GROUP, count)
        d_scores = (
            (probs * (d_probs - delta[:, :, None]))
            .astype(jnp.bfloat16)
            .reshape(tokens * GROUP, count)
        )
        value_part = contract_first(probs_low, out_flat)
        key_part = contract_first(d_scores, query_flat)
        grad_rows = jnp.dot(d_scores, keys, preferred_element_type=jnp.float32)
        return (grad_rows, key_part, value_part)

    def grad_skipped(grad_rows):
        blank = jnp.zeros((count, keys.shape[1]), jnp.float32)
        return (grad_rows, blank, blank)

    return lax.cond(jnp.any(mask), grad_compute, grad_skipped, grad_rows)


def body(query, key, value, d_out, seg_blocks, seg_audio):
    key, value = (
        lax.all_to_all(key, "head", split_axis=1, concat_axis=0, tiled=True),
        lax.all_to_all(value, "head", split_axis=1, concat_axis=0, tiled=True),
    )
    rows = query.shape[0]
    half = rows // 2
    place = lax.axis_index("ctx")
    scale = 1.0 / math.sqrt(DH)
    keys = key[:, 0, :]
    values = value[:, 0, :]
    own_pos = place * rows + jnp.arange(rows, dtype=jnp.int32)
    first = prepare(query[:half], d_out[:half], own_pos[:half], seg_blocks, seg_audio)
    second = prepare(query[half:], d_out[half:], own_pos[half:], seg_blocks, seg_audio)
    groups = (first, second)
    blank_stats = jnp.zeros((half, GROUP), jnp.float32)
    start_stats = tuple(
        (
            (jnp.full((half, GROUP), NEG, jnp.float32), blank_stats, blank_stats)
            for group_data in groups
        )
    )
    piece = (
        lax.all_gather(keys, "ctx", axis=0, tiled=True),
        lax.all_gather(values, "ctx", axis=0, tiled=True),
    )
    stats = tuple(
        (
            stats_group(group_data, state, piece, seg_blocks, seg_audio)
            for group_data, state in zip(groups, start_stats)
        )
    )
    finals = tuple(
        ((highest + jnp.log(total), weighted / total) for highest, total, weighted in stats)
    )
    blank_rows = jnp.zeros((half * GROUP, DH), jnp.float32)
    piece = (
        lax.all_gather(keys, "ctx", axis=0, tiled=True),
        lax.all_gather(values, "ctx", axis=0, tiled=True),
    )
    grad_list = (blank_rows, blank_rows)
    piece_keys = piece[0]
    count = piece_keys.shape[0]
    key_sum = jnp.zeros((count, DH), jnp.float32)
    value_sum = jnp.zeros((count, DH), jnp.float32)
    new_rows = []
    for group_data, group_finals, grad_rows in zip(groups, finals, grad_list):
        grad_rows, key_part, value_part = grad_group(
            group_data, group_finals, grad_rows, piece, seg_blocks, seg_audio
        )
        key_sum = key_sum + key_part
        value_sum = value_sum + value_part
        new_rows.append(grad_rows)
    update = jnp.stack([key_sum, value_sum], axis=1)
    key_grad = update
    grads = (key_grad, tuple(new_rows))
    key_grad, grad_list = grads
    summed = lax.psum_scatter(key_grad, "ctx", scatter_dimension=0, tiled=True)
    d_key = (summed[:, 0, :] * scale).astype(jnp.bfloat16)[:, None, :]
    d_value = summed[:, 1, :].astype(jnp.bfloat16)[:, None, :]
    first_rows = (grad_list[0] * scale).astype(jnp.bfloat16).reshape(half, GROUP, DH)
    second_rows = (grad_list[1] * scale).astype(jnp.bfloat16).reshape(half, GROUP, DH)
    d_query = jnp.concatenate([first_rows, second_rows], axis=0)
    d_key, d_value = (
        lax.all_to_all(d_key, "head", split_axis=0, concat_axis=1, tiled=True),
        lax.all_to_all(d_value, "head", split_axis=0, concat_axis=1, tiled=True),
    )
    return (d_query, d_key, d_value)


def fused_kernel(
    n, heads, q_hbm, do_hbm, k_hbm, v_hbm, blocks_hbm, audio_hbm,
    dq_ref, dk_ref, dv_ref,
    q_ref, do_ref, k_ref, v_ref, blocks_ref, audio_ref, q_turned, do_turned,
    head_out, kv, p_s, dp_s, ds_s, m_s, l_s, w_s, own_part,
    gy_out, gy_in, gz_out, gz_in,
    in_sem, kvz_send, kvz_recv, kvy_send, kvy_recv,
    gy_send, gy_recv, gz_send, gz_recv,
):
    chain = n // 2
    place = lax.axis_index("ctx")
    head = lax.axis_index("head")
    a, b = place // 2, lax.rem(place, 2)
    rows_flat = q_ref.shape[0]
    rows = rows_flat // GROUP
    part = rows // heads
    scale = 1.0 / math.sqrt(DH)
    power = scale * math.log2(math.e)
    inner = scale / OUTER
    chunk = min(ROW_CHUNK, rows_flat)
    chunks = [slice(r, r + chunk) for r in range(0, rows_flat, chunk)]

    def head_peer(d):
        return lax.rem(head + d, heads)

    def up(d):
        return lax.rem(a + d, chain)

    def down(d):
        return lax.rem(a + chain - d, chain)

    def at(ctx_index, head_index):
        return (ctx_index, head_index)

    partner = 2 * a + 1 - b

    def send(src, dst, send_sem, recv_sem, target):
        return pltpu.make_async_remote_copy(
            src_ref=src, dst_ref=dst, send_sem=send_sem, recv_sem=recv_sem,
            device_id=target, device_id_type=MESH,
        )

    pairs = [(da, dh) for da in range(chain) for dh in range(heads)]
    others = pairs[1:]

    barrier = pltpu.get_barrier_semaphore()
    for da, dh in others:
        pl.semaphore_signal(
            barrier, inc=1, device_id=at(2 * up(da) + b, head_peer(dh)), device_id_type=MESH
        )
    pl.semaphore_signal(barrier, inc=1, device_id=at(partner, head), device_id_type=MESH)

    loads = [
        pltpu.make_async_copy(src, dst, in_sem.at[i])
        for i, (src, dst) in enumerate((
            (k_hbm, k_ref), (v_hbm, v_ref), (blocks_hbm, blocks_ref),
            (audio_hbm, audio_ref), (q_hbm, q_ref), (do_hbm, do_ref),
        ))
    ]
    for load in loads:
        load.start()
    loads[0].wait()
    loads[1].wait()
    for i in range(heads):
        head_out[i, 0] = k_ref[:, i, :]
        head_out[i, 1] = v_ref[:, i, :]
    pl.semaphore_wait(barrier, chain * heads)

    mine = pl.ds(pl.multiple_of(head * part, part), part)

    def chain_copy(da, dh):
        peer = head_peer(dh)
        return send(
            head_out.at[peer], kv.at[place, :, mine, :], kvz_send.at[da * heads + dh],
            kvz_recv.at[a * heads + head], at(2 * up(da) + b, peer),
        )

    def chain_arrival(d, dh):
        source, peer = down(d), head_peer(dh)
        theirs = pl.ds(pl.multiple_of(peer * part, part), part)
        return send(
            head_out.at[peer], kv.at[2 * source + b, :, theirs, :], kvz_send.at[0],
            kvz_recv.at[source * heads + peer], at(partner, head),
        )

    def relay_copy(d):
        slot = 2 * down(d) + b
        return send(kv.at[slot], kv.at[slot], kvy_send.at[d], kvy_recv.at[down(d)], at(partner, head))

    def relay_arrival(d):
        slot = 2 * down(d) + 1 - b
        return send(kv.at[slot], kv.at[slot], kvy_send.at[d], kvy_recv.at[down(d)], at(partner, head))

    for da, dh in others:
        chain_copy(da, dh).start()
    kv[place, :, mine, :] = head_out[head]

    for load in loads[2:]:
        load.wait()
    q_turned[...] = q_ref[...].T
    do_turned[...] = do_ref[...].T

    pos = place * rows + lax.broadcasted_iota(jnp.int32, (1, rows_flat), 1) // GROUP
    limit = pos + 1
    start = jnp.int32(0)
    for s in range(blocks_ref.shape[0]):
        end = start + blocks_ref[s] * BLK
        inside = (pos >= start) & (pos < end) & (jnp.broadcast_to(audio_ref[s], pos.shape) == 1)
        limit = jnp.where(inside, end, limit)
        start = end

    for dh in range(1, heads):
        chain_arrival(0, dh).wait_recv()
    relay_copy(0).start()

    key_pos = lax.broadcasted_iota(jnp.int32, (rows, 1), 0)

    def stats_step(t, carry):
        d = lax.rem(t, chain)
        own_column = t < chain
        slot = 2 * down(d) + lax.rem(b + t // chain, 2)

        @pl.when(own_column & (t > 0))
        def _():
            for dh in range(heads):
                chain_arrival(d, dh).wait_recv()
            relay_copy(d).start()

        @pl.when(jnp.logical_not(own_column))
        def _():
            relay_arrival(d).wait_recv()

        keys, values = kv[slot, 0], kv[slot, 1]
        s_all = jnp.dot(keys, q_turned[...], preferred_element_type=jnp.float32)
        dp_all = jnp.dot(values, do_turned[...], preferred_element_type=jnp.float32)
        bound = limit - slot * rows
        found = []
        for c in chunks:
            s = jnp.where(key_pos < bound[:, c], s_all[:, c], NEG)
            high = jnp.max(s, axis=0, keepdims=True)
            p = jnp.exp2((s - high) * power)
            total = jnp.sum(p, axis=0, keepdims=True)
            weighted = jnp.sum(p * dp_all[:, c], axis=0, keepdims=True)
            found.append((p, high, total, weighted))
        dp_s[slot] = dp_all
        for c, (p, high, total, weighted) in zip(chunks, found):
            p_s[slot, :, c] = p
            m_s[slot, :, c] = high
            l_s[slot, :, c] = total
            w_s[slot, :, c] = weighted
        return carry

    lax.fori_loop(0, n, stats_step, 0)

    m_all = m_s[...]
    high = jnp.max(m_all, axis=0)
    factors = jnp.exp2((m_all - high[None]) * power)
    total = jnp.sum(factors * l_s[...], axis=0)
    delta = jnp.sum(factors * w_s[...], axis=0) / total
    m_s[...] = factors / total[None]

    def pair_copy(d):
        dest = down(d)
        return send(gy_out.at[d], gy_in.at[dest], gy_send.at[d], gy_recv.at[dest], at(partner, head))

    def sum_copy(d, dh):
        peer = head_peer(dh)
        theirs = pl.ds(pl.multiple_of(peer * part, part), part)
        return send(
            gz_out.at[d, :, theirs, :], gz_in.at[a * heads + head], gz_send.at[d * heads + dh],
            gz_recv.at[a * heads + head], at(2 * down(d) + b, peer),
        )

    def sum_arrival(da, dh):
        index = up(da) * heads + head_peer(dh)
        return send(
            gz_out.at[0, :, mine, :], gz_in.at[index], gz_send.at[0], gz_recv.at[index], at(partner, head)
        )

    def combine(d):
        pair_copy(d).wait_recv()
        return own_part[d] + gy_in[down(d)].astype(jnp.float32)

    def grad_step(t, carry):
        d = chain - 1 - lax.rem(t, chain)
        other_column = t < chain
        slot = 2 * down(d) + lax.rem(b + t // chain + 1, 2)
        probs_low, ds = [], []
        for c in chunks:
            probs = p_s[slot, :, c] * m_s[slot, :, c]
            probs_low.append(probs.astype(jnp.bfloat16))
            ds.append((probs * (dp_s[slot, :, c] - delta[:, c])).astype(jnp.bfloat16))
        probs_low, ds = jnp.concatenate(probs_low, axis=1), jnp.concatenate(ds, axis=1)
        value_part = jnp.dot(probs_low, do_ref[...], preferred_element_type=jnp.float32)
        key_part = jnp.dot(ds, q_ref[...], preferred_element_type=jnp.float32)
        ds_s[slot] = ds

        @pl.when(other_column)
        def _():
            gy_out[d, 0] = key_part.astype(jnp.bfloat16)
            gy_out[d, 1] = value_part.astype(jnp.bfloat16)
            pair_copy(d).start()

        @pl.when(jnp.logical_not(other_column))
        def _():
            own_part[d, 0] = key_part
            own_part[d, 1] = value_part

        @pl.when(jnp.logical_not(other_column) & (d > 0))
        def _():
            gz_out[d] = combine(d).astype(jnp.bfloat16)
            for dh in range(heads):
                sum_copy(d, dh).start()

        return carry

    lax.fori_loop(0, n, grad_step, 0)

    all_keys = kv[:, 0].reshape(n * rows, DH)

    def query_rows(c):
        all_ds = ds_s[:, :, c].reshape(n * rows, c.stop - c.start)
        dq_ref[c, :] = (contract_first(all_keys, all_ds) * inner).T.astype(jnp.bfloat16)

    middle = rows_flat // 2
    query_rows(slice(0, middle))
    gz_out[0] = combine(0).astype(jnp.bfloat16)
    for dh in range(1, heads):
        sum_copy(0, dh).start()
    gz_in[a * heads + head] = gz_out[0, :, mine, :]
    query_rows(slice(middle, rows_flat))

    for da, dh in others:
        sum_arrival(da, dh).wait_recv()
    for i in range(heads):
        acc = gz_in[i].astype(jnp.float32)
        for source in range(1, chain):
            acc = acc + gz_in[source * heads + i].astype(jnp.float32)
        dk_ref[:, i, :] = (acc[0] * inner).astype(jnp.bfloat16)
        dv_ref[:, i, :] = (acc[1] / OUTER).astype(jnp.bfloat16)

    for da, dh in others:
        chain_copy(da, dh).wait_send()
        sum_copy(da, dh).wait_send()
    for d in range(chain):
        relay_copy(d).wait_send()
        pair_copy(d).wait_send()


def fused_scratch(n, heads, rows, segments):
    flat, chain, part = rows * GROUP, n // 2, rows // heads
    low, full, sem = jnp.bfloat16, jnp.float32, pltpu.SemaphoreType.DMA
    return [
        pltpu.VMEM((flat, DH), low),
        pltpu.VMEM((flat, DH), low),
        pltpu.VMEM((part, heads, DH), low),
        pltpu.VMEM((part, heads, DH), low),
        pltpu.SMEM((segments,), jnp.int32),
        pltpu.SMEM((segments,), jnp.int32),
        pltpu.VMEM((DH, flat), low),
        pltpu.VMEM((DH, flat), low),
        pltpu.VMEM((heads, 2, part, DH), low),
        pltpu.VMEM((n, 2, rows, DH), low),
        pltpu.VMEM((n, rows, flat), full),
        pltpu.VMEM((n, rows, flat), full),
        pltpu.VMEM((n, rows, flat), low),
        pltpu.VMEM((n, 1, flat), full),
        pltpu.VMEM((n, 1, flat), full),
        pltpu.VMEM((n, 1, flat), full),
        pltpu.VMEM((chain, 2, rows, DH), full),
        pltpu.VMEM((chain, 2, rows, DH), low),
        pltpu.VMEM((chain, 2, rows, DH), low),
        pltpu.VMEM((chain, 2, rows, DH), low),
        pltpu.VMEM((chain * heads, 2, part, DH), low),
        sem((6,)), sem((chain * heads,)), sem((chain * heads,)), sem((chain,)), sem((chain,)),
        sem((chain,)), sem((chain,)), sem((chain * heads,)), sem((chain * heads,)),
    ]


def fused_body(n, heads, query, key, value, d_out, seg_blocks, seg_audio):
    rows = query.shape[0]
    flat = rows * GROUP
    low = jnp.bfloat16
    vmem, hbm = pl.BlockSpec(memory_space=pltpu.VMEM), pl.BlockSpec(memory_space=pltpu.HBM)
    d_query, d_key, d_value = pl.pallas_call(
        functools.partial(fused_kernel, n, heads),
        out_shape=[
            jax.ShapeDtypeStruct((flat, DH), low),
            jax.ShapeDtypeStruct(key.shape, low),
            jax.ShapeDtypeStruct(value.shape, low),
        ],
        in_specs=[hbm] * 6,
        out_specs=[vmem] * 3,
        scratch_shapes=fused_scratch(n, heads, rows, seg_blocks.shape[0]),
        cost_estimate=pl.CostEstimate(
            flops=10 * n * rows * flat * DH, bytes_accessed=6 * flat * DH, transcendentals=n * rows * flat
        ),
        compiler_params=pltpu.CompilerParams(
            collective_id=0, has_side_effects=True, vmem_limit_bytes=VMEM_BUDGET
        ),
    )(query.reshape(flat, DH), d_out.reshape(flat, DH), key, value, seg_blocks, seg_audio)
    d_query = d_query.reshape(query.shape)
    return tuple(grad * jnp.asarray(OUTER, low) for grad in (d_query, d_key, d_value))


def plan_body(n, heads, query, key, value, d_out, seg_blocks, seg_audio):
    rows = query.shape[0]
    held = n * rows * rows * GROUP * 10
    if held > VMEM_BUDGET // 2 or n % 2 or query.shape[1] != GROUP or key.shape[1] != heads:
        return body(query, key, value, d_out, seg_blocks, seg_audio)
    return fused_body(n, heads, query, key, value, d_out, seg_blocks, seg_audio)


def solution(mesh):
    placed = (
        P("ctx", "head", None),
        P(("ctx", "head"), None, None),
        P(("ctx", "head"), None, None),
        P("ctx", "head", None),
        P(),
        P(),
    )
    return jax.shard_map(
        functools.partial(plan_body, mesh.shape["ctx"], mesh.shape["head"]),
        mesh=mesh,
        in_specs=placed,
        out_specs=(
            P("ctx", "head", None),
            P(("ctx", "head"), None, None),
            P(("ctx", "head"), None, None),
        ),
        check_vma=False,
    )
```
